128 devices in a mesh: blk: 16 (over z, y_hi, core), uly: 8 (over x, y_lo).
Axes of the slice: x: 4, y: 4 (y_hi: 2, y_lo: 2; y = y_hi * 2 + y_lo), z: 4, core: 2. Of those that a mesh axis runs over, the one named last changes fastest.
Arguments:
- queries: bfloat16 [128, 192, 8192], P(('blk', 'uly')), may hold values from -4 to 4
- own_keys: bfloat16 [128, 192, 1024], P(('blk', 'uly')), may hold values from -12 to 12
- own_values: bfloat16 [128, 192, 1024], P(('blk', 'uly')), may hold values from -6 to 6
- key_codes: bfloat16 [2048, 1024], P('blk', 'uly'), may hold values from -128 to 128
- value_codes: bfloat16 [2048, 1024], P('blk', 'uly'), may hold values from -6 to 6
- code_scales: bfloat16 [2048, 8, 2], P('blk', 'uly'), may hold values from 0.5 to 2
- lengths: int32 [128], P(('blk', 'uly')), may hold values from 1 to 192, as said below
Outputs:
- attention_out: bfloat16 [128, 192, 8192], P(('blk', 'uly'))
The draws below stay inside these ranges and needn't reach their ends.
Inputs may be any that keep to these rules, and one draw needn't show every extreme that they name: `lengths`: one response in every draw has exactly 192 tokens.
All inputs are finite; a program needn't handle non-finite values.
Results may differ from the reference program's by a relative error of at most 0.0056.
Values may be sent and summed in bfloat16 or wider, within the bound.
A program may use at most 192 MiB of HBM per device.

```python
import math
import jax
import jax.numpy as jnp
from jax import lax

D_HEAD = 128
HEADS = 64
KV_HEADS = 8
LENGTH = 192
PROMPT = 2048
SLOTS = 128


def base_queries(key):
    return jnp.clip(jax.random.normal(key, (SLOTS, LENGTH, HEADS * D_HEAD), jnp.float32), -4.0, 4.0)


def base_factors(key):
    factor_key = jax.random.fold_in(key, 12)
    spread = jax.random.uniform(factor_key, (PROMPT, KV_HEADS, 2), jnp.float32, math.log(0.5), math.log(2.0))
    return jnp.exp(spread)


def draw_queries(key, part):
    return base_queries(key).astype(jnp.bfloat16)


def draw_key_codes(key, part):
    factors = base_factors(key)
    own_key = jax.random.fold_in(key, 11)
    entries = jnp.clip(2.0 * jax.random.normal(own_key, (PROMPT, KV_HEADS * D_HEAD), jnp.float32), -8.0, 8.0)
    codes_all = entries / jnp.repeat(factors[:, :, 0], D_HEAD, axis=1)
    return codes_all.astype(jnp.bfloat16)


def draw_code_scales(key, part):
    factors = base_factors(key)
    return factors.astype(jnp.bfloat16)


def draw_lengths(key, part):
    own_key = jax.random.fold_in(key, 13)
    first_key, second_key, third_key = jax.random.split(own_key, 3)
    drawn = jax.random.randint(first_key, (SLOTS,), 1, LENGTH + 1, jnp.int32)
    longest = jax.random.randint(second_key, (), 0, SLOTS, jnp.int32)
    shortest = (longest + jax.random.randint(third_key, (), 1, SLOTS, jnp.int32)) % SLOTS
    drawn = drawn.at[longest].set(LENGTH)
    return drawn.at[shortest].set(1)


def level_of(stream_key, extent, cuts, low, high):
    def one(axis_at, blocks):
        heights = jax.random.uniform(jax.random.fold_in(jax.random.fold_in(stream_key, 6), axis_at), (blocks,), jnp.float32, low / len(cuts), high / len(cuts))
        return jnp.repeat(jnp.exp(heights), extent[axis_at] // blocks).reshape((-1,) + (1,) * (len(extent) - axis_at - 1))

    level = one(*cuts[0])
    for cut in cuts[1:]:
        level = level * one(*cut)
    return level


def normal_values(stream_key, dims, deviation, limit, cuts=(), kind=jnp.bfloat16):
    loudness = level_of(stream_key, dims, cuts, -0.22, 0.18) if cuts else 1.0
    entries = jax.random.normal(stream_key, dims, jnp.float32) * deviation * loudness
    return jnp.minimum(jnp.maximum(entries, -limit), limit).astype(kind)


def setup_inputs(seed: int = 0) -> dict:
    splits = jax.random.split(jax.random.key(seed), 8)
    return {
        "queries": draw_queries(jax.random.fold_in(splits[7], 71), 0),
        "own_keys": normal_values(splits[1], (SLOTS, LENGTH, KV_HEADS * D_HEAD), 3.0, 12.0, ((0, 128),)),
        "own_values": normal_values(splits[2], (SLOTS, LENGTH, KV_HEADS * D_HEAD), 1.0, 6.0, ((0, 128),)),
        "key_codes": draw_key_codes(jax.random.fold_in(splits[7], 71), 0),
        "value_codes": normal_values(splits[4], (PROMPT, KV_HEADS * D_HEAD), 1.0, 6.0, ((0, 16), (1, 8))),
        "code_scales": draw_code_scales(jax.random.fold_in(splits[7], 71), 0),
        "lengths": draw_lengths(jax.random.fold_in(splits[7], 71), 0),
    }


def reference(queries, own_keys, own_values, key_codes, value_codes, code_scales, lengths):
    group_size = HEADS // KV_HEADS
    inverse_root = 1.0 / math.sqrt(D_HEAD)
    factors = code_scales.astype(jnp.float32)
    prompt_keys = (key_codes.astype(jnp.float32).reshape(PROMPT, KV_HEADS, D_HEAD) * factors[:, :, 0:1]).astype(jnp.bfloat16)
    prompt_values = (value_codes.astype(jnp.float32).reshape(PROMPT, KV_HEADS, D_HEAD) * factors[:, :, 1:2]).astype(jnp.bfloat16)
    positions = jnp.arange(LENGTH, dtype=jnp.int32)
    causal = positions[:, None] >= positions[None, :]
    causal_tiled = jnp.tile(causal, (group_size, 1))
    query_tokens = jnp.tile(positions, group_size)

    def attend_one(indices):
        slot_index = indices[0]
        head_index = indices[1]
        slot_query = lax.dynamic_index_in_dim(queries, slot_index, 0, keepdims=False)
        query_group = lax.dynamic_slice_in_dim(slot_query, head_index * group_size * D_HEAD, group_size * D_HEAD, 1)
        query_group = query_group.reshape(LENGTH, group_size, D_HEAD).transpose(1, 0, 2).reshape(group_size * LENGTH, D_HEAD)
        key_block = lax.dynamic_index_in_dim(prompt_keys, head_index, 1, keepdims=False)
        value_block = lax.dynamic_index_in_dim(prompt_values, head_index, 1, keepdims=False)
        slot_keys = lax.dynamic_index_in_dim(own_keys, slot_index, 0, keepdims=False)
        slot_values = lax.dynamic_index_in_dim(own_values, slot_index, 0, keepdims=False)
        own_key = lax.dynamic_slice_in_dim(slot_keys, head_index * D_HEAD, D_HEAD, 1)
        own_value = lax.dynamic_slice_in_dim(slot_values, head_index * D_HEAD, D_HEAD, 1)
        prompt_scores = jnp.dot(query_group, key_block.T, preferred_element_type=jnp.float32) * inverse_root
        own_scores = jnp.dot(query_group, own_key.T, preferred_element_type=jnp.float32) * inverse_root
        highest = jnp.maximum(lax.optimization_barrier(jnp.max(prompt_scores, axis=1)), lax.optimization_barrier(jnp.max(jnp.where(causal_tiled, own_scores, -jnp.inf), axis=1)))
        prompt_weights = jnp.exp(prompt_scores - highest[:, None])
        own_weights = jnp.where(causal_tiled, jnp.exp(own_scores - highest[:, None]), 0.0)
        totals = lax.optimization_barrier(jnp.sum(prompt_weights, axis=1)) + lax.optimization_barrier(jnp.sum(own_weights, axis=1))
        numerator = jnp.dot(prompt_weights.astype(jnp.bfloat16), value_block, preferred_element_type=jnp.float32)
        numerator = numerator + jnp.dot(own_weights.astype(jnp.bfloat16), own_value, preferred_element_type=jnp.float32)
        result = numerator / totals[:, None]
        length_here = lax.dynamic_index_in_dim(lengths, slot_index, 0, keepdims=False)
        result = jnp.where((query_tokens < length_here)[:, None], result, 0.0)
        return result.reshape(group_size, LENGTH, D_HEAD).transpose(1, 0, 2).reshape(LENGTH, group_size * D_HEAD)
    slot_list = jnp.repeat(jnp.arange(SLOTS, dtype=jnp.int32), KV_HEADS)
    group_list = jnp.tile(jnp.arange(KV_HEADS, dtype=jnp.int32), SLOTS)
    outputs = lax.map(attend_one, jnp.stack([slot_list, group_list], axis=1))
    outputs = outputs.reshape(SLOTS, KV_HEADS, LENGTH, group_size * D_HEAD).transpose(0, 2, 1, 3)
    return outputs.reshape(SLOTS, LENGTH, HEADS * D_HEAD).astype(jnp.bfloat16)
```

```python
import math

import jax
import jax.numpy as jnp
from jax import lax
from jax.experimental import pallas as pl
from jax.experimental.pallas import tpu as pltpu
from jax.sharding import PartitionSpec as P

D = 128
HEADS_KV = 8
GROUP = 8
LENGTH = 192
BLOCKS = 16
PROMPT = 2048
CHUNK = 512
TOKENS = 64
HALF = 4
ROWS = HALF * TOKENS
SCALE = math.log2(math.e) / math.sqrt(D)


def dot_t(a, b):
    return lax.dot_general(a, b, (((1,), (1,)), ((), ())), preferred_element_type=jnp.float32)


def attend(lengths_ref, q_ref, kv_ref, ok_ref, ov_ref, o_ref, s_ref, m_ref, ovt_ref, mask_ref):
    key_at = lax.broadcasted_iota(jnp.int32, (TOKENS, ROWS), 0)
    token_at = lax.broadcasted_iota(jnp.int32, (TOKENS, ROWS), 1) % TOKENS
    mask_ref[...] = jnp.where(token_at >= key_at, 0.0, -jnp.inf).astype(jnp.float32)
    for g in range(HEADS_KV):
        turned = ov_ref[:, g * D : (g + 1) * D].T
        ovt_ref[g] = jnp.concatenate([turned, jnp.zeros((D, 256 - LENGTH), jnp.bfloat16)], axis=1)
    length = lengths_ref[0]
    per = CHUNK // D

    def columns(g, hh, h):
        return pl.ds(pl.multiple_of((g * GROUP + hh * HALF + h) * D, D), D)

    def scores(g, t, slot):
        hh, j = t // 3, t % 3
        q = jnp.concatenate([q_ref[j * TOKENS : (j + 1) * TOKENS, columns(g, hh, h)] for h in range(HALF)], axis=0)
        q = q.astype(jnp.float32) * SCALE
        high = q.astype(jnp.bfloat16)
        low = (q - high.astype(jnp.float32)).astype(jnp.bfloat16)
        q = jnp.concatenate([high, low], axis=1)
        top = jnp.full((8, ROWS), -jnp.inf, jnp.float32)
        for c in range(PROMPT // CHUNK):
            keys = jnp.concatenate([kv_ref[g * BLOCKS + c * per + b, :D] for b in range(per)], axis=0)
            s = dot_t(jnp.concatenate([keys, keys], axis=1), q)
            s_ref[slot, c * CHUNK : (c + 1) * CHUNK] = s
            top = jnp.maximum(top, jnp.max(s.reshape(CHUNK // 8, 8, ROWS), axis=0))
        n = (j + 1) * TOKENS
        keys = ok_ref[:n, pl.ds(pl.multiple_of(g * D, D), D)]
        s = dot_t(jnp.concatenate([keys, keys], axis=1), q)
        if j:
            s_ref[slot, PROMPT : PROMPT + j * TOKENS] = s[: j * TOKENS]
            top = jnp.maximum(top, jnp.max(s[: j * TOKENS].reshape(j * 8, 8, ROWS), axis=0))
        last = s[j * TOKENS :] + mask_ref[...]
        s_ref[slot, PROMPT + j * TOKENS : PROMPT + n] = last
        top = jnp.maximum(top, jnp.max(last.reshape(8, 8, ROWS), axis=0))
        m_ref[slot] = jnp.broadcast_to(jnp.max(top, axis=0, keepdims=True), (8, ROWS))

    def values(g, t, slot):
        hh, j = t // 3, t % 3
        top = m_ref[slot][:1]
        total = jnp.zeros((8, ROWS), jnp.float32)
        acc = jnp.zeros((D, ROWS), jnp.float32)
        for c in range(PROMPT // CHUNK):
            p = jnp.exp2(s_ref[slot, c * CHUNK : (c + 1) * CHUNK] - top)
            total = total + jnp.sum(p.reshape(CHUNK // 8, 8, ROWS), axis=0)
            turned = jnp.concatenate([kv_ref[g * BLOCKS + c * per + b, D:] for b in range(per)], axis=1)
            acc = acc + jnp.dot(turned, p.astype(jnp.bfloat16), preferred_element_type=jnp.float32)
        n = (j + 1) * TOKENS
        depth = 128 if j < 2 else 256
        p = jnp.exp2(s_ref[slot, PROMPT : PROMPT + n] - top)
        total = total + jnp.sum(p.reshape(n // 8, 8, ROWS), axis=0)
        p = p.astype(jnp.bfloat16)
        if depth > n:
            p = jnp.concatenate([p, jnp.zeros((depth - n, ROWS), jnp.bfloat16)], axis=0)
        acc = acc + jnp.dot(ovt_ref[g, :, :depth], p, preferred_element_type=jnp.float32)
        token = lax.broadcasted_iota(jnp.int32, (1, ROWS), 1) % TOKENS + j * TOKENS
        factor = jnp.where(token < length, 1.0 / jnp.sum(total, axis=0, keepdims=True), 0.0)
        out = (acc * factor).T.astype(jnp.bfloat16)
        for h in range(HALF):
            o_ref[j * TOKENS : (j + 1) * TOKENS, columns(g, hh, h)] = out[h * TOKENS : (h + 1) * TOKENS]

    scores(0, 0, 0)

    def head(g, carry):
        for t in range(6):
            if t < 5:
                scores(g, t + 1, (t + 1) % 2)
            else:
                scores(jnp.minimum(g + 1, HEADS_KV - 1), 0, 0)
            values(g, t, t % 2)
        return carry

    lax.fori_loop(0, HEADS_KV, head, 0)


def body(queries, own_keys, own_values, key_codes, value_codes, code_scales, lengths):
    factors = code_scales.astype(jnp.float32)
    keys = (key_codes.astype(jnp.float32) * factors[:, :, 0]).astype(jnp.bfloat16)
    values = (value_codes.astype(jnp.float32) * factors[:, :, 1]).astype(jnp.bfloat16)
    shard = jnp.concatenate([keys, values.T], axis=0)
    prompt = lax.all_gather(shard[None], "blk", axis=0, tiled=True)
    prompt = lax.all_gather(prompt, "uly", axis=0, tiled=True)
    vmem = pl.BlockSpec(memory_space=pltpu.VMEM)
    out = pl.pallas_call(
        attend,
        out_shape=jax.ShapeDtypeStruct((LENGTH, HEADS_KV * GROUP * D), jnp.bfloat16),
        in_specs=[pl.BlockSpec(memory_space=pltpu.SMEM)] + [vmem] * 4,
        out_specs=vmem,
        scratch_shapes=[
            pltpu.VMEM((2, PROMPT + 256, ROWS), jnp.float32),
            pltpu.VMEM((2, 8, ROWS), jnp.float32),
            pltpu.VMEM((HEADS_KV, D, 256), jnp.bfloat16),
            pltpu.VMEM((TOKENS, ROWS), jnp.float32),
        ],
        compiler_params=pltpu.CompilerParams(vmem_limit_bytes=60 * 2**20),
        cost_estimate=pl.CostEstimate(flops=14_000_000_000, bytes_accessed=16_000_000, transcendentals=27_000_000),
    )(lengths, queries[0], prompt, own_keys[0], own_values[0])
    return out[None]


def solution(mesh):
    placed = (
        P(("blk", "uly"), None, None),
        P(("blk", "uly"), None, None),
        P(("blk", "uly"), None, None),
        P("blk", "uly"),
        P("blk", "uly"),
        P("blk", "uly", None),
        P(("blk", "uly")),
    )
    return jax.shard_map(
        body, mesh=mesh, in_specs=placed, out_specs=P(("blk", "uly"), None, None), check_vma=False
    )
```

```python
import math

import jax
import jax.numpy as jnp
from jax import lax
from jax.experimental import pallas as pl
from jax.experimental.pallas import tpu as pltpu
from jax.sharding import PartitionSpec as P

MESH = pl.DeviceIdType.MESH
D = 128
HEADS_KV = 8
GROUP = 8
LENGTH = 192
CHUNK = 512
PROMPT = 2048
TOKENS = 64
HALF = 4
ROWS = HALF * TOKENS
TILES = 6
SCALE = math.log2(math.e) / math.sqrt(D)
STEPS = (2, 1, 3)


def dot_t(a, b):
    return lax.dot_general(a, b, (((1,), (1,)), ((), ())), preferred_element_type=jnp.float32)


def attend(
    scales_ref, kc_ref, vc_ref, lengths_ref, q_hbm, ok_hbm, ov_hbm, out_hbm,
    q_ref, ok_ref, ov_ref, o_ref, kbuf, vbuf, s_ref, m_ref, ovt_ref, mask_ref, acc_ref, state_ref,
    in_sem, out_sem, x_send, x_recv, k1_send, k1_recv, v1_send, v1_recv,
    k2_send, k2_recv, v2_send, v2_recv, sk_send, sk_recv, sv_send, sv_recv,
):
    blk = lax.axis_index("blk")
    uly = lax.axis_index("uly")
    x, yl = uly // 2, uly % 2
    z, yh, core = blk // 4, (blk // 2) % 2, blk % 2
    y = yh * 2 + yl
    other = 1 - core

    def device(xx, yy, zz, cc):
        return (zz * 4 + (yy // 2) * 2 + cc, xx * 2 + yy % 2)

    def along_x(d):
        return device((x + d) % 4, y, z, core)

    def along_y(d):
        return device(x, (y + d) % 4, z, core)

    def along_z(d):
        return device(x, y, (z + d) % 4, core)

    sibling = device(x, y, z, other)

    def plane(p):
        return (x + p + p // 2 - 2 * (p // 3)) % 4

    barrier = pltpu.get_barrier_semaphore()
    for d in STEPS:
        for to in (along_x(d), along_y(d), along_z(d)):
            pl.semaphore_signal(barrier, inc=1, device_id=to, device_id_type=MESH)
    pl.semaphore_signal(barrier, inc=1, device_id=sibling, device_id_type=MESH)

    loads = [
        pltpu.make_async_copy(a, b, in_sem.at[i])
        for i, (a, b) in enumerate(((ok_hbm, ok_ref), (ov_hbm, ov_ref), (q_hbm, q_ref)))
    ]
    for load in loads:
        load.start()

    factors = scales_ref[...].astype(jnp.float32)
    turned = kc_ref[...].astype(jnp.float32).T * factors[0:1]
    kbuf[x, yl, core, z, yh] = turned.T.astype(jnp.bfloat16)
    turned = vc_ref[...].astype(jnp.float32).T * factors[1:2]
    vbuf[x, yl, core, yh, z] = turned.astype(jnp.bfloat16)

    pl.semaphore_wait(barrier, 10)

    def move(ref, send, recv, to):
        return pltpu.make_async_remote_copy(
            src_ref=ref, dst_ref=ref, send_sem=send, recv_sem=recv, device_id=to, device_id_type=MESH
        )

    def x_moves(i):
        d = (1, 3, 2)[i]
        back = (4 - d) % 4
        out = [
            move(kbuf.at[x, yl, core, z, yh], x_send.at[i, 0], x_recv.at[i, 0], along_x(back)),
            move(vbuf.at[x, yl, core, yh, z], x_send.at[i, 1], x_recv.at[i, 1], along_x(back)),
        ]
        return out

    def x_arrival(p):
        xp = plane(p)
        return [
            move(kbuf.at[xp, yl, core, z, yh], x_send.at[p - 1, 0], x_recv.at[p - 1, 0], sibling),
            move(vbuf.at[xp, yl, core, yh, z], x_send.at[p - 1, 1], x_recv.at[p - 1, 1], sibling),
        ]

    def first_out(p):
        xp = plane(p)
        out = []
        for i, d in enumerate(STEPS):
            out.append(move(kbuf.at[xp, yl, core, z, yh], k1_send.at[p, i], k1_recv.at[p, i], along_y(d)))
            out.append(move(vbuf.at[xp, yl, core, yh, z], v1_send.at[p, i], v1_recv.at[p, i], along_z(d)))
        return out

    def k1_in(p, i):
        xp = plane(p)
        ys = (y + 4 - STEPS[i]) % 4
        return move(kbuf.at[xp, ys % 2, core, z, ys // 2], k1_send.at[p, i], k1_recv.at[p, i], sibling)

    def v1_in(p, i):
        xp = plane(p)
        zs = (z + 4 - STEPS[i]) % 4
        return move(vbuf.at[xp, yl, core, yh, zs], v1_send.at[p, i], v1_recv.at[p, i], sibling)

    def head(a):
        return yl if a == 0 else 1 - yl

    def k2_out(p, a, i):
        xp = plane(p)
        return move(kbuf.at[xp, head(a), core, z], k2_send.at[p, a, i], k2_recv.at[p, a, i], along_z(STEPS[i]))

    def k2_in(p, a, i):
        xp = plane(p)
        zs = (z + 4 - STEPS[i]) % 4
        return move(kbuf.at[xp, head(a), core, zs], k2_send.at[p, a, i], k2_recv.at[p, a, i], sibling)

    def v2_out(p, i):
        xp = plane(p)
        return move(vbuf.at[xp, yl, core, yh], v2_send.at[p, i], v2_recv.at[p, i], along_y(STEPS[i]))

    def v2_in(p, i):
        xp = plane(p)
        ys = (y + 4 - STEPS[i]) % 4
        return move(vbuf.at[xp, ys % 2, core, ys // 2], v2_send.at[p, i], v2_recv.at[p, i], sibling)

    def sk_out(p, a, i):
        xp = plane(p)
        zs = z if i == 3 else (z + 4 - STEPS[i]) % 4
        return move(kbuf.at[xp, head(a), core, zs], sk_send.at[p, a, i], sk_recv.at[p, a, i], sibling)

    def sk_in(p, a, i):
        xp = plane(p)
        zs = z if i == 3 else (z + 4 - STEPS[i]) % 4
        return move(kbuf.at[xp, head(a), other, zs], sk_send.at[p, a, i], sk_recv.at[p, a, i], sibling)

    def sv_out(p, i):
        xp = plane(p)
        ys = y if i == 3 else (y + 4 - STEPS[i]) % 4
        return move(vbuf.at[xp, ys % 2, core, ys // 2], sv_send.at[p, i], sv_recv.at[p, i], sibling)

    def sv_in(p, i):
        xp = plane(p)
        ys = y if i == 3 else (y + 4 - STEPS[i]) % 4
        return move(vbuf.at[xp, ys % 2, other, ys // 2], sv_send.at[p, i], sv_recv.at[p, i], sibling)

    def start_first(p):
        for c in first_out(p):
            c.start()

    def start_second(p):
        k1_in(p, 0).wait_recv()
        for i in range(3):
            k2_out(p, 0, i).start()
        sk_out(p, 0, 3).start()
        for i in range(3):
            v1_in(p, i).wait_recv()
        for i in range(3):
            v2_out(p, i).start()
        sv_out(p, 3).start()
        for i in (1, 2):
            k1_in(p, i).wait_recv()
        for i in range(3):
            k2_out(p, 1, i).start()
        sk_out(p, 1, 3).start()

    def share_own(p):
        for i in (1, 2, 0):
            k2_in(p, 0, i).wait_recv()
            sk_out(p, 0, i).start()
        v2_in(p, 0).wait_recv()
        sv_out(p, 0).start()

    def share_other(p):
        for i in (1, 2, 0):
            k2_in(p, 1, i).wait_recv()
            sk_out(p, 1, i).start()
        for i in (1, 2):
            v2_in(p, i).wait_recv()
            sv_out(p, i).start()

    def have_own(p):
        for i in range(4):
            sk_in(p, 0, i).wait_recv()
        for i in (0, 3):
            sv_in(p, i).wait_recv()

    def have_other(p):
        for i in range(4):
            sk_in(p, 1, i).wait_recv()
        for i in (1, 2):
            sv_in(p, i).wait_recv()

    start_first(0)
    for i in range(3):
        for c in x_moves(i):
            c.start()

    key_at = lax.broadcasted_iota(jnp.int32, (TOKENS, ROWS), 0)
    token_at = lax.broadcasted_iota(jnp.int32, (TOKENS, ROWS), 1) % TOKENS
    mask_ref[...] = jnp.where(token_at >= key_at, 0.0, -jnp.inf).astype(jnp.float32)
    length = lengths_ref[0]

    def columns(g, hh, h):
        return pl.ds(pl.multiple_of((g * GROUP + hh * HALF + h) * D, D), D)

    def queries(g, t):
        hh, j = t // 3, t % 3
        q = jnp.concatenate([q_ref[j * TOKENS : (j + 1) * TOKENS, columns(g, hh, h)] for h in range(HALF)], axis=0)
        q = q.astype(jnp.float32) * SCALE
        high = q.astype(jnp.bfloat16)
        low = (q - high.astype(jnp.float32)).astype(jnp.bfloat16)
        return jnp.concatenate([high, low], axis=1)

    def own_part(g, t):
        j = t % 3
        n = (j + 1) * TOKENS
        keys = ok_ref[:n, pl.ds(pl.multiple_of(g * D, D), D)]
        s = dot_t(jnp.concatenate([keys, keys], axis=1), queries(g, t))
        last = s[j * TOKENS :] + mask_ref[...]
        s = jnp.concatenate([s[: j * TOKENS], last], axis=0) if j else last
        top = jnp.max(s, axis=0, keepdims=True)
        p = jnp.exp2(s - top)
        total = jnp.sum(p.reshape(n // 8, 8, ROWS), axis=0)
        depth = 128 if j < 2 else 256
        p = p.astype(jnp.bfloat16)
        if depth > n:
            p = jnp.concatenate([p, jnp.zeros((depth - n, ROWS), jnp.bfloat16)], axis=0)
        acc_ref[g * TILES + t] = jnp.dot(ovt_ref[g, :, :depth], p, preferred_element_type=jnp.float32)
        state_ref[g * TILES + t, 0] = jnp.broadcast_to(top, (8, ROWS))
        state_ref[g * TILES + t, 1] = total

    def own_head(g, carry):
        cols = pl.ds(pl.multiple_of(g * D, D), D)
        ovt_ref[g] = jnp.concatenate([ov_ref[:, cols].T, jnp.zeros((D, 256 - LENGTH), jnp.bfloat16)], axis=1)
        for t in range(TILES):
            own_part(g, t)
        return carry

    def key_blocks(xp, hd):
        return [kbuf[xp, hd, c, zz, hh] for c in range(2) for zz in range(4) for hh in range(2)]

    def value_blocks(xp, hd):
        return [vbuf[xp, hd, c, hh, zz] for c in range(2) for zz in range(4) for hh in range(2)]

    per = CHUNK // D

    def scores(p, a, t, slot):
        xp, hd = plane(p), head(a)
        g = xp * 2 + hd
        q = queries(g, t)
        blocks = key_blocks(xp, hd)
        top = state_ref[g * TILES + t, 0]
        for c in range(PROMPT // CHUNK):
            keys = jnp.concatenate(blocks[c * per : (c + 1) * per], axis=0)
            s = dot_t(jnp.concatenate([keys, keys], axis=1), q)
            s_ref[slot, c * CHUNK : (c + 1) * CHUNK] = s
            top = jnp.maximum(top, jnp.max(s.reshape(CHUNK // 8, 8, ROWS), axis=0))
        m_ref[slot] = jnp.broadcast_to(jnp.max(top, axis=0, keepdims=True), (8, ROWS))

    def values(p, a, t, slot):
        xp, hd = plane(p), head(a)
        g = xp * 2 + hd
        hh, j = t // 3, t % 3
        blocks = value_blocks(xp, hd)
        top = m_ref[slot]
        shrink = jnp.exp2(state_ref[g * TILES + t, 0] - top)
        total = state_ref[g * TILES + t, 1] * shrink
        acc = acc_ref[g * TILES + t] * shrink[:1]
        for c in range(PROMPT // CHUNK):
            w = jnp.exp2(s_ref[slot, c * CHUNK : (c + 1) * CHUNK] - top[:1])
            total = total + jnp.sum(w.reshape(CHUNK // 8, 8, ROWS), axis=0)
            turned = jnp.concatenate(blocks[c * per : (c + 1) * per], axis=1)
            acc = acc + jnp.dot(turned, w.astype(jnp.bfloat16), preferred_element_type=jnp.float32)
        token = lax.broadcasted_iota(jnp.int32, (1, ROWS), 1) % TOKENS + j * TOKENS
        factor = jnp.where(token < length, 1.0 / jnp.sum(total, axis=0, keepdims=True), 0.0)
        out = (acc * factor).T.astype(jnp.bfloat16)
        for h in range(HALF):
            o_ref[j * TOKENS : (j + 1) * TOKENS, columns(g, hh, h)] = out[h * TOKENS : (h + 1) * TOKENS]

    def out_copy(p, a):
        g = plane(p) * 2 + head(a)
        cols = pl.ds(pl.multiple_of(g * GROUP * D, GROUP * D), GROUP * D)
        return pltpu.make_async_copy(o_ref.at[:, cols], out_hbm.at[:, cols], out_sem.at[p, a])

    for load in loads:
        load.wait()
    lax.fori_loop(0, 4, own_head, 0)
    start_second(0)
    lax.fori_loop(4, HEADS_KV, own_head, 0)
    share_own(0)
    for c in x_arrival(1):
        c.wait_recv()
    start_first(1)
    have_own(0)
    scores(0, 0, 0, 0)

    def work(p, final):
        for u in range(2 * TILES):
            a, t = u // TILES, u % TILES
            if u == 2:
                share_other(p)
            if u == 3 and not final:
                start_second(p + 1)
            if u == 5:
                have_other(p)
            if u == 8 and not final:
                share_own(p + 1)
            if u == 9 and not final:
                @pl.when(p < 2)
                def _():
                    for c in x_arrival(p + 2):
                        c.wait_recv()
                    start_first(p + 2)
            if u == 11 and not final:
                have_own(p + 1)
            if u < 11:
                scores(p, (u + 1) // TILES, (u + 1) % TILES, (u + 1) % 2)
            elif not final:
                scores(p + 1, 0, 0, 0)
            values(p, a, t, u % 2)
            if t == TILES - 1:
                out_copy(p, a).start()

    def planes(p, carry):
        work(p, False)
        return carry

    lax.fori_loop(0, 3, planes, 0)
    work(3, True)

    for i in range(3):
        for c in x_moves(i):
            c.wait_send()

    def settle(p, carry):
        for c in first_out(p):
            c.wait_send()
        for i in range(3):
            for a in range(2):
                k2_out(p, a, i).wait_send()
            v2_out(p, i).wait_send()
        for i in range(4):
            for a in range(2):
                sk_out(p, a, i).wait_send()
            sv_out(p, i).wait_send()
        for a in range(2):
            out_copy(p, a).wait()
        return carry

    lax.fori_loop(0, 4, settle, 0)


def body(queries, own_keys, own_values, key_codes, value_codes, code_scales, lengths):
    scales = jnp.transpose(code_scales[:, 0, :])
    vmem = pl.BlockSpec(memory_space=pltpu.VMEM)
    hbm = pl.BlockSpec(memory_space=pl.ANY)
    dma = pltpu.SemaphoreType.DMA
    width = HEADS_KV * GROUP * D
    out = pl.pallas_call(
        attend,
        out_shape=jax.ShapeDtypeStruct((LENGTH, width), jnp.bfloat16),
        in_specs=[vmem, vmem, vmem, pl.BlockSpec(memory_space=pltpu.SMEM), hbm, hbm, hbm],
        out_specs=hbm,
        scratch_shapes=[
            pltpu.VMEM((LENGTH, width), jnp.bfloat16),
            pltpu.VMEM((LENGTH, HEADS_KV * D), jnp.bfloat16),
            pltpu.VMEM((LENGTH, HEADS_KV * D), jnp.bfloat16),
            pltpu.VMEM((LENGTH, width), jnp.bfloat16),
            pltpu.VMEM((4, 2, 2, 4, 2, D, D), jnp.bfloat16),
            pltpu.VMEM((4, 2, 2, 2, 4, D, D), jnp.bfloat16),
            pltpu.VMEM((2, PROMPT, ROWS), jnp.float32),
            pltpu.VMEM((2, 8, ROWS), jnp.float32),
            pltpu.VMEM((HEADS_KV, D, 256), jnp.bfloat16),
            pltpu.VMEM((TOKENS, ROWS), jnp.float32),
            pltpu.VMEM((HEADS_KV * TILES, D, ROWS), jnp.float32),
            pltpu.VMEM((HEADS_KV * TILES, 2, 8, ROWS), jnp.float32),
            dma((3,)), dma((4, 2)),
            dma((3, 2)), dma((3, 2)),
            dma((4, 3)), dma((4, 3)),
            dma((4, 3)), dma((4, 3)),
            dma((4, 2, 3)), dma((4, 2, 3)),
            dma((4, 3)), dma((4, 3)),
            dma((4, 2, 4)), dma((4, 2, 4)),
            dma((4, 4)), dma((4, 4)),
        ],
        compiler_params=pltpu.CompilerParams(
            collective_id=0, has_side_effects=True, vmem_limit_bytes=56 * 2**20
        ),
        cost_estimate=pl.CostEstimate(flops=14_000_000_000, bytes_accessed=8_000_000, transcendentals=27_000_000),
    )(scales, key_codes, value_codes, lengths, queries[0], own_keys[0], own_values[0])
    return out[None]


def solution(mesh):
    placed = (
        P(("blk", "uly"), None, None),
        P(("blk", "uly"), None, None),
        P(("blk", "uly"), None, None),
        P("blk", "uly"),
        P("blk", "uly"),
        P("blk", "uly", None),
        P(("blk", "uly")),
    )
    return jax.shard_map(
        body, mesh=mesh, in_specs=placed, out_specs=P(("blk", "uly"), None, None), check_vma=False
    )
```

```python
import math

import jax
import jax.numpy as jnp
from jax import lax
from jax.experimental import pallas as pl
from jax.experimental.pallas import tpu as pltpu
from jax.sharding import PartitionSpec as P

MESH = pl.DeviceIdType.MESH
D = 128
HEADS_KV = 8
GROUP = 8
LENGTH = 192
CHUNK = 512
PROMPT = 2048
TOKENS = 64
HALF = 4
ROWS = HALF * TOKENS
TILES = 6
SCALE = math.log2(math.e) / math.sqrt(D)
STEPS = (2, 1, 3)
NEAR = 96


def dot_t(a, b):
    return lax.dot_general(a, b, (((1,), (1,)), ((), ())), preferred_element_type=jnp.float32)


def attend(
    scales_hbm, kc_hbm, vc_hbm, lengths_ref, q_hbm, ok_hbm, ov_hbm, o_ref,
    kc_ref, vc_ref, scales_ref, q_ref, ok_ref, ov_ref, kbuf, vbuf, s_ref, m_ref, mask_ref, acc_ref, state_ref,
    in_sem, x_send, x_recv, far_send, far_recv, k1_send, k1_recv, v1_send, v1_recv,
    k2_send, k2_recv, v2_send, v2_recv, sk_send, sk_recv, sv_send, sv_recv, share_send, share_recv,
):
    blk = lax.axis_index("blk")
    uly = lax.axis_index("uly")
    x, yl = uly // 2, uly % 2
    z, yh, core = blk // 4, (blk // 2) % 2, blk % 2
    y = yh * 2 + yl
    other = 1 - core

    def device(xx, yy, zz, cc):
        return (zz * 4 + (yy // 2) * 2 + cc, xx * 2 + yy % 2)

    def along_x(d):
        return device((x + d) % 4, y, z, core)

    def along_y(d):
        return device(x, (y + d) % 4, z, core)

    def along_z(d):
        return device(x, y, (z + d) % 4, core)

    sibling = device(x, y, z, other)

    def plane(p):
        return (x + p + p // 2 - 2 * (p // 3)) % 4

    barrier = pltpu.get_barrier_semaphore()
    for d in STEPS:
        for to in (along_x(d), along_y(d), along_z(d)):
            pl.semaphore_signal(barrier, inc=1, device_id=to, device_id_type=MESH)
    pl.semaphore_signal(barrier, inc=1, device_id=sibling, device_id_type=MESH)

    loads = [
        pltpu.make_async_copy(a, b, in_sem.at[i])
        for i, (a, b) in enumerate(
            (
                (scales_hbm, scales_ref), (kc_hbm, kc_ref), (vc_hbm, vc_ref),
                (ok_hbm, ok_ref), (ov_hbm, ov_ref), (q_hbm, q_ref),
            )
        )
    ]
    for load in loads:
        load.start()
    for load in loads[:3]:
        load.wait()

    factors = scales_ref[...].astype(jnp.float32)
    turned = kc_ref[...].astype(jnp.float32).T * factors[0:1]
    kbuf[x, yl, core, z, yh] = turned.T.astype(jnp.bfloat16)
    turned = vc_ref[...].astype(jnp.float32).T * factors[1:2]
    vbuf[x, yl, core, yh, z] = turned.astype(jnp.bfloat16)

    pl.semaphore_wait(barrier, 10)

    def move(ref, send, recv, to):
        return pltpu.make_async_remote_copy(
            src_ref=ref, dst_ref=ref, send_sem=send, recv_sem=recv, device_id=to, device_id_type=MESH
        )

    def rows(p):
        return pl.ds(0, D if isinstance(p, int) and p == 0 else NEAR)

    far = pl.ds(NEAR, D - NEAR)

    def head(a):
        return yl if a == 0 else 1 - yl

    def y_of(i):
        return (y + 4 - STEPS[i]) % 4

    def z_of(i):
        return (z + 4 - STEPS[i]) % 4

    def x_out(i):
        to = along_x((3, 1, 2)[i])
        return [
            move(kbuf.at[x, yl, core, z, yh, pl.ds(0, NEAR)], x_send.at[i, 0], x_recv.at[i, 0], to),
            move(vbuf.at[x, yl, core, yh, z, pl.ds(0, NEAR)], x_send.at[i, 1], x_recv.at[i, 1], to),
        ]

    def x_in(p):
        xp = plane(p)
        return [
            move(kbuf.at[xp, yl, core, z, yh, pl.ds(0, NEAR)], x_send.at[p - 1, 0], x_recv.at[p - 1, 0], sibling),
            move(vbuf.at[xp, yl, core, yh, z, pl.ds(0, NEAR)], x_send.at[p - 1, 1], x_recv.at[p - 1, 1], sibling),
        ]

    def far_out(i, a):
        to = along_x((3, 1, 2)[i])
        return [
            move(kbuf.at[x, head(a), core, :, :, far], far_send.at[i, a, 0], far_recv.at[i, a, 0], to),
            move(vbuf.at[x, head(a), core, :, :, far], far_send.at[i, a, 1], far_recv.at[i, a, 1], to),
        ]

    def far_in(p, a):
        xp = plane(p)
        return [
            move(kbuf.at[xp, head(a), core, :, :, far], far_send.at[p - 1, a, 0], far_recv.at[p - 1, a, 0], sibling),
            move(vbuf.at[xp, head(a), core, :, :, far], far_send.at[p - 1, a, 1], far_recv.at[p - 1, a, 1], sibling),
        ]

    def first_out(p):
        xp = plane(p)
        out = []
        for i, d in enumerate(STEPS):
            out.append(move(kbuf.at[xp, yl, core, z, yh, rows(p)], k1_send.at[p, i], k1_recv.at[p, i], along_y(d)))
            out.append(move(vbuf.at[xp, yl, core, yh, z, rows(p)], v1_send.at[p, i], v1_recv.at[p, i], along_z(d)))
        return out

    def k1_in(p, i):
        ys = y_of(i)
        return move(kbuf.at[plane(p), ys % 2, core, z, ys // 2, rows(p)], k1_send.at[p, i], k1_recv.at[p, i], sibling)

    def v1_in(p, i):
        return move(vbuf.at[plane(p), yl, core, yh, z_of(i), rows(p)], v1_send.at[p, i], v1_recv.at[p, i], sibling)

    def k2_out(p, a, i):
        return move(kbuf.at[plane(p), head(a), core, z, :, rows(p)], k2_send.at[p, a, i], k2_recv.at[p, a, i], along_z(STEPS[i]))

    def k2_in(p, a, i):
        return move(kbuf.at[plane(p), head(a), core, z_of(i), :, rows(p)], k2_send.at[p, a, i], k2_recv.at[p, a, i], sibling)

    def v2_out(p, i):
        return move(vbuf.at[plane(p), yl, core, yh, :, rows(p)], v2_send.at[p, i], v2_recv.at[p, i], along_y(STEPS[i]))

    def v2_in(p, i):
        ys = y_of(i)
        return move(vbuf.at[plane(p), ys % 2, core, ys // 2, :, rows(p)], v2_send.at[p, i], v2_recv.at[p, i], sibling)

    def sk(a, i, c):
        return move(kbuf.at[x, head(a), c, z if i == 3 else z_of(i)], sk_send.at[a, i], sk_recv.at[a, i], sibling)

    def sv(i, c):
        ys = y if i == 3 else y_of(i)
        return move(vbuf.at[x, ys % 2, c, ys // 2], sv_send.at[i], sv_recv.at[i], sibling)

    def share(p, a, c):
        xp = plane(p)
        return [
            move(kbuf.at[xp, head(a), c], share_send.at[p - 1, a, 0], share_recv.at[p - 1, a, 0], sibling),
            move(vbuf.at[xp, head(a), c], share_send.at[p - 1, a, 1], share_recv.at[p - 1, a, 1], sibling),
        ]

    def start(copies):
        for c in copies:
            c.start()

    def arrive(copies):
        for c in copies:
            c.wait_recv()

    def start_first(p):
        if not (isinstance(p, int) and p == 0):
            arrive(x_in(p))
        start(first_out(p))

    def second_own(p):
        near = isinstance(p, int) and p == 0
        k1_in(p, 0).wait_recv()
        start([k2_out(p, 0, i) for i in range(3)])
        if near:
            sk(0, 3, core).start()
        arrive([v1_in(p, i) for i in range(3)])
        v2_out(p, 0).start()
        if near:
            sv(3, core).start()
        arrive([k1_in(p, i) for i in (1, 2)])
        if near:
            sk(1, 3, core).start()

    def second_other(p):
        start([k2_out(p, 1, i) for i in range(3)])
        start([v2_out(p, i) for i in (1, 2)])

    def start_second(p):
        second_own(p)
        second_other(p)

    def share_first(a):
        for i in (1, 2, 0):
            k2_in(0, a, i).wait_recv()
            sk(a, i, core).start()
        for i in ((0,), (1, 2))[a]:
            v2_in(0, i).wait_recv()
            sv(i, core).start()
        for i in range(3):
            start(far_out(i, a))

    def have_first(a):
        arrive([sk(a, i, other) for i in range(4)])
        arrive([sv(i, other) for i in ((0, 3), (1, 2))[a]])

    def share_later(p, a):
        arrive([k2_in(p, a, i) for i in (1, 2, 0)])
        kf, vf = far_in(p, a)
        kf.wait_recv()
        ks, vs = share(p, a, core)
        ks.start()
        arrive([v2_in(p, i) for i in ((0,), (1, 2))[a]])
        vf.wait_recv()
        vs.start()

    def have_later(p, a):
        arrive(share(p, a, other))

    start_first(0)
    for i in range(3):
        start(x_out(i))

    key_at = lax.broadcasted_iota(jnp.int32, (TOKENS, ROWS), 0)
    token_at = lax.broadcasted_iota(jnp.int32, (TOKENS, ROWS), 1) % TOKENS
    mask_ref[...] = jnp.where(token_at >= key_at, 0.0, -jnp.inf).astype(jnp.float32)
    length = lengths_ref[0]

    def columns(g, hh, h):
        return pl.ds(pl.multiple_of((g * GROUP + hh * HALF + h) * D, D), D)

    def queries(g, t):
        hh, j = t // 3, t % 3
        q = jnp.concatenate([q_ref[j * TOKENS : (j + 1) * TOKENS, columns(g, hh, h)] for h in range(HALF)], axis=0)
        q = q.astype(jnp.float32) * SCALE
        high = q.astype(jnp.bfloat16)
        low = (q - high.astype(jnp.float32)).astype(jnp.bfloat16)
        return jnp.concatenate([high, low], axis=1)

    def own_head(g, carry):
        cols = pl.ds(pl.multiple_of(g * D, D), D)
        turned = ov_ref[:, cols].T
        keys = ok_ref[:, cols]
        keys = jnp.concatenate([keys, keys], axis=1)
        mask = mask_ref[...]
        scored = []
        for t in range(TILES):
            j = t % 3
            s = dot_t(keys[: (j + 1) * TOKENS], queries(g, t))
            last = s[j * TOKENS :] + mask
            scored.append(jnp.concatenate([s[: j * TOKENS], last], axis=0) if j else last)
        weighed = []
        for t in range(TILES):
            n = (t % 3 + 1) * TOKENS
            s = scored[t]
            top = jnp.max(s, axis=0, keepdims=True)
            p = jnp.exp2(s - top)
            state_ref[g * TILES + t, 0] = jnp.broadcast_to(top, (8, ROWS))
            state_ref[g * TILES + t, 1] = jnp.sum(p.reshape(n // 8, 8, ROWS), axis=0)
            weighed.append(p.astype(jnp.bfloat16))
        for t in range(TILES):
            n = (t % 3 + 1) * TOKENS
            acc_ref[g * TILES + t] = jnp.dot(turned[:, :n], weighed[t], preferred_element_type=jnp.float32)
        return carry

    def key_blocks(xp, hd):
        return [kbuf[xp, hd, c, zz, hh] for c in range(2) for zz in range(4) for hh in range(2)]

    def value_blocks(xp, hd):
        return [vbuf[xp, hd, c, hh, zz] for c in range(2) for zz in range(4) for hh in range(2)]

    per = CHUNK // D

    def scores(p, a, t, slot):
        xp, hd = plane(p), head(a)
        g = xp * 2 + hd
        q = queries(g, t)
        blocks = key_blocks(xp, hd)
        top = state_ref[g * TILES + t, 0]
        for c in range(PROMPT // CHUNK):
            keys = jnp.concatenate(blocks[c * per : (c + 1) * per], axis=0)
            s = dot_t(jnp.concatenate([keys, keys], axis=1), q)
            s_ref[slot, c * CHUNK : (c + 1) * CHUNK] = s
            top = jnp.maximum(top, jnp.max(s.reshape(CHUNK // 8, 8, ROWS), axis=0))
        m_ref[slot] = jnp.broadcast_to(jnp.max(top, axis=0, keepdims=True), (8, ROWS))

    def values(p, a, t, slot):
        xp, hd = plane(p), head(a)
        g = xp * 2 + hd
        hh, j = t // 3, t % 3
        blocks = value_blocks(xp, hd)
        top = m_ref[slot]
        shrink = jnp.exp2(state_ref[g * TILES + t, 0] - top)
        total = state_ref[g * TILES + t, 1] * shrink
        acc = acc_ref[g * TILES + t] * shrink[:1]
        for c in range(PROMPT // CHUNK):
            w = jnp.exp2(s_ref[slot, c * CHUNK : (c + 1) * CHUNK] - top[:1])
            total = total + jnp.sum(w.reshape(CHUNK // 8, 8, ROWS), axis=0)
            turned = jnp.concatenate(blocks[c * per : (c + 1) * per], axis=1)
            acc = acc + jnp.dot(turned, w.astype(jnp.bfloat16), preferred_element_type=jnp.float32)
        token = lax.broadcasted_iota(jnp.int32, (1, ROWS), 1) % TOKENS + j * TOKENS
        factor = jnp.where(token < length, 1.0 / jnp.sum(total, axis=0, keepdims=True), 0.0)
        out = (acc * factor).T.astype(jnp.bfloat16)
        for h in range(HALF):
            o_ref[j * TOKENS : (j + 1) * TOKENS, columns(g, hh, h)] = out[h * TOKENS : (h + 1) * TOKENS]

    for load in loads[3:]:
        load.wait()
    lax.fori_loop(0, 2, own_head, 0)
    second_own(0)
    start_first(1)
    lax.fori_loop(2, 5, own_head, 0)
    share_first(0)
    second_other(0)
    lax.fori_loop(5, HEADS_KV, own_head, 0)
    second_own(1)
    have_first(0)
    scores(0, 0, 0, 0)

    def work(p, place):
        for u in range(2 * TILES):
            a, t = u // TILES, u % TILES
            if place == 0:
                if u == 0:
                    start_first(2)
                    start_first(3)
                if u == 2:
                    second_other(1)
                if u == 3:
                    share_first(1)
                if u == 5:
                    have_first(1)
                    start_second(2)
                if u == 9:
                    start_second(3)
            else:
                if u == 1:
                    share_later(p, 1)
                if u == 5:
                    have_later(p, 1)
            if place < 2 and u == 7:
                share_later(p + 1, 0)
            if place < 2 and u == 11:
                have_later(p + 1, 0)
            if u < 11:
                scores(p, (u + 1) // TILES, (u + 1) % TILES, (u + 1) % 2)
            elif place < 2:
                scores(p + 1, 0, 0, 0)
            values(p, a, t, u % 2)

    def planes(p, carry):
        work(p, 1)
        return carry

    work(0, 0)
    lax.fori_loop(1, 3, planes, 0)
    work(3, 2)

    def sent(copies):
        for c in copies:
            c.wait_send()

    def settle(p):
        sent(first_out(p))
        for i in range(3):
            sent([k2_out(p, a, i) for a in range(2)])
            v2_out(p, i).wait_send()

    for i in range(3):
        sent(x_out(i))
        for a in range(2):
            sent(far_out(i, a))
    for i in range(4):
        sent([sk(0, i, core), sk(1, i, core), sv(i, core)])
    settle(0)

    def settle_later(p, carry):
        settle(p)
        for a in range(2):
            sent(share(p, a, core))
        return carry

    lax.fori_loop(1, 4, settle_later, 0)


def body(queries, own_keys, own_values, key_codes, value_codes, code_scales, lengths):
    scales = jnp.transpose(code_scales[:, 0, :])
    vmem = pl.BlockSpec(memory_space=pltpu.VMEM)
    hbm = pl.BlockSpec(memory_space=pl.ANY)
    dma = pltpu.SemaphoreType.DMA
    width = HEADS_KV * GROUP * D
    out = pl.pallas_call(
        attend,
        out_shape=pltpu.VMEM((LENGTH, width), jnp.bfloat16),
        in_specs=[hbm, hbm, hbm, pl.BlockSpec(memory_space=pltpu.SMEM), hbm, hbm, hbm],
        out_specs=vmem,
        scratch_shapes=[
            pltpu.VMEM((D, D), jnp.bfloat16),
            pltpu.VMEM((D, D), jnp.bfloat16),
            pltpu.VMEM((2, D), jnp.bfloat16),
            pltpu.VMEM((LENGTH, width), jnp.bfloat16),
            pltpu.VMEM((LENGTH, HEADS_KV * D), jnp.bfloat16),
            pltpu.VMEM((LENGTH, HEADS_KV * D), jnp.bfloat16),
            pltpu.VMEM((4, 2, 2, 4, 2, D, D), jnp.bfloat16),
            pltpu.VMEM((4, 2, 2, 2, 4, D, D), jnp.bfloat16),
            pltpu.VMEM((2, PROMPT, ROWS), jnp.float32),
            pltpu.VMEM((2, 8, ROWS), jnp.float32),
            pltpu.VMEM((TOKENS, ROWS), jnp.float32),
            pltpu.VMEM((HEADS_KV * TILES, D, ROWS), jnp.float32),
            pltpu.VMEM((HEADS_KV * TILES, 2, 8, ROWS), jnp.float32),
            dma((6,)),
            dma((3, 2)), dma((3, 2)),
            dma((3, 2, 2)), dma((3, 2, 2)),
            dma((4, 3)), dma((4, 3)),
            dma((4, 3)), dma((4, 3)),
            dma((4, 2, 3)), dma((4, 2, 3)),
            dma((4, 3)), dma((4, 3)),
            dma((2, 4)), dma((2, 4)),
            dma((4,)), dma((4,)),
            dma((3, 2, 2)), dma((3, 2, 2)),
        ],
        compiler_params=pltpu.CompilerParams(
            collective_id=0, has_side_effects=True, vmem_limit_bytes=56 * 2**20
        ),
        cost_estimate=pl.CostEstimate(flops=14_000_000_000, bytes_accessed=8_000_000, transcendentals=27_000_000),
    )(scales, key_codes, value_codes, lengths, queries[0], own_keys[0], own_values[0])
    return out[None]


def solution(mesh):
    placed = (
        P(("blk", "uly"), None, None),
        P(("blk", "uly"), None, None),
        P(("blk", "uly"), None, None),
        P("blk", "uly"),
        P("blk", "uly"),
        P("blk", "uly", None),
        P(("blk", "uly")),
    )
    return jax.shard_map(
        body, mesh=mesh, in_specs=placed, out_specs=P(("blk", "uly"), None, None), check_vma=False
    )
```

```python
import math

import jax
import jax.numpy as jnp
from jax import lax
from jax.experimental import pallas as pl
from jax.experimental.pallas import tpu as pltpu
from jax.sharding import PartitionSpec as P

MESH = pl.DeviceIdType.MESH
D = 128
HEADS_KV = 8
GROUP = 8
LENGTH = 192
CHUNK = 512
PROMPT = 2048
TOKENS = 64
HALF = 4
ROWS = HALF * TOKENS
TILES = 6
SCALE = math.log2(math.e) / math.sqrt(D)
STEPS = (2, 1, 3)
NEAR = 64


def dot_t(a, b):
    return lax.dot_general(a, b, (((1,), (1,)), ((), ())), preferred_element_type=jnp.float32)


def attend(
    scales_hbm, kc_hbm, vc_hbm, lengths_ref, q_hbm, ok_hbm, ov_hbm, o_ref,
    kc_ref, vc_ref, scales_ref, q_ref, ok_ref, ov_ref, kbuf, vbuf, s_ref, m_ref, mask_ref, acc_ref, state_ref,
    in_sem, x_send, x_recv, far_send, far_recv, k1_send, k1_recv, v1_send, v1_recv,
    k2_send, k2_recv, v2_send, v2_recv, sk_send, sk_recv, sv_send, sv_recv, share_send, share_recv,
):
    blk = lax.axis_index("blk")
    uly = lax.axis_index("uly")
    x, yl = uly // 2, uly % 2
    z, yh, core = blk // 4, (blk // 2) % 2, blk % 2
    y = yh * 2 + yl
    other = 1 - core

    def device(xx, yy, zz, cc):
        return (zz * 4 + (yy // 2) * 2 + cc, xx * 2 + yy % 2)

    def along_x(d):
        return device((x + d) % 4, y, z, core)

    def along_y(d):
        return device(x, (y + d) % 4, z, core)

    def along_z(d):
        return device(x, y, (z + d) % 4, core)

    sibling = device(x, y, z, other)

    def plane(p):
        return (x + p + p // 2 - 2 * (p // 3)) % 4

    barrier = pltpu.get_barrier_semaphore()
    for d in STEPS:
        for to in (along_x(d), along_y(d), along_z(d)):
            pl.semaphore_signal(barrier, inc=1, device_id=to, device_id_type=MESH)
    pl.semaphore_signal(barrier, inc=1, device_id=sibling, device_id_type=MESH)

    loads = [
        pltpu.make_async_copy(a, b, in_sem.at[i])
        for i, (a, b) in enumerate(
            (
                (scales_hbm, scales_ref), (kc_hbm, kc_ref), (vc_hbm, vc_ref),
                (ok_hbm, ok_ref), (ov_hbm, ov_ref), (q_hbm, q_ref),
            )
        )
    ]
    for load in loads:
        load.start()
    for load in loads[:3]:
        load.wait()

    factors = scales_ref[...].astype(jnp.float32)
    turned = kc_ref[...].astype(jnp.float32).T * factors[0:1]
    kbuf[x, yl, core, z, yh] = turned.T.astype(jnp.bfloat16)
    turned = vc_ref[...].astype(jnp.float32).T * factors[1:2]
    vbuf[x, yl, core, yh, z] = turned.astype(jnp.bfloat16)

    pl.semaphore_wait(barrier, 10)

    def move(ref, send, recv, to):
        return pltpu.make_async_remote_copy(
            src_ref=ref, dst_ref=ref, send_sem=send, recv_sem=recv, device_id=to, device_id_type=MESH
        )

    def rows(p):
        return pl.ds(0, D if isinstance(p, int) and p % 3 == 0 else NEAR)

    far = pl.ds(NEAR, D - NEAR)

    def head(a):
        return yl if a == 0 else 1 - yl

    def y_of(i):
        return (y + 4 - STEPS[i]) % 4

    def z_of(i):
        return (z + 4 - STEPS[i]) % 4

    def x_out(i):
        to = along_x((3, 1, 2)[i])
        return [
            move(kbuf.at[x, yl, core, z, yh, rows(i + 1)], x_send.at[i, 0], x_recv.at[i, 0], to),
            move(vbuf.at[x, yl, core, yh, z, rows(i + 1)], x_send.at[i, 1], x_recv.at[i, 1], to),
        ]

    def x_in(p):
        xp = plane(p)
        return [
            move(kbuf.at[xp, yl, core, z, yh, rows(p)], x_send.at[p - 1, 0], x_recv.at[p - 1, 0], sibling),
            move(vbuf.at[xp, yl, core, yh, z, rows(p)], x_send.at[p - 1, 1], x_recv.at[p - 1, 1], sibling),
        ]

    def far_out(i, a):
        to = along_x((3, 1, 2)[i])
        return [
            move(kbuf.at[x, head(a), core, :, :, far], far_send.at[i, a, 0], far_recv.at[i, a, 0], to),
            move(vbuf.at[x, head(a), core, :, :, far], far_send.at[i, a, 1], far_recv.at[i, a, 1], to),
        ]

    def far_in(p, a):
        xp = plane(p)
        return [
            move(kbuf.at[xp, head(a), core, :, :, far], far_send.at[p - 1, a, 0], far_recv.at[p - 1, a, 0], sibling),
            move(vbuf.at[xp, head(a), core, :, :, far], far_send.at[p - 1, a, 1], far_recv.at[p - 1, a, 1], sibling),
        ]

    def first_out(p):
        xp = plane(p)
        out = []
        for i, d in enumerate(STEPS):
            out.append(move(kbuf.at[xp, yl, core, z, yh, rows(p)], k1_send.at[p, i], k1_recv.at[p, i], along_y(d)))
            out.append(move(vbuf.at[xp, yl, core, yh, z, rows(p)], v1_send.at[p, i], v1_recv.at[p, i], along_z(d)))
        return out

    def k1_in(p, i):
        ys = y_of(i)
        return move(kbuf.at[plane(p), ys % 2, core, z, ys // 2, rows(p)], k1_send.at[p, i], k1_recv.at[p, i], sibling)

    def v1_in(p, i):
        return move(vbuf.at[plane(p), yl, core, yh, z_of(i), rows(p)], v1_send.at[p, i], v1_recv.at[p, i], sibling)

    def k2_out(p, a, i):
        return move(kbuf.at[plane(p), head(a), core, z, :, rows(p)], k2_send.at[p, a, i], k2_recv.at[p, a, i], along_z(STEPS[i]))

    def k2_in(p, a, i):
        return move(kbuf.at[plane(p), head(a), core, z_of(i), :, rows(p)], k2_send.at[p, a, i], k2_recv.at[p, a, i], sibling)

    def v2_out(p, i):
        return move(vbuf.at[plane(p), yl, core, yh, :, rows(p)], v2_send.at[p, i], v2_recv.at[p, i], along_y(STEPS[i]))

    def v2_in(p, i):
        ys = y_of(i)
        return move(vbuf.at[plane(p), ys % 2, core, ys // 2, :, rows(p)], v2_send.at[p, i], v2_recv.at[p, i], sibling)

    def sk(a, i, c):
        return move(kbuf.at[x, head(a), c, z if i == 3 else z_of(i)], sk_send.at[a, i], sk_recv.at[a, i], sibling)

    def sv(i, c):
        ys = y if i == 3 else y_of(i)
        return move(vbuf.at[x, ys % 2, c, ys // 2], sv_send.at[i], sv_recv.at[i], sibling)

    def share(p, a, c):
        xp = plane(p)
        return [
            move(kbuf.at[xp, head(a), c], share_send.at[p - 1, a, 0], share_recv.at[p - 1, a, 0], sibling),
            move(vbuf.at[xp, head(a), c], share_send.at[p - 1, a, 1], share_recv.at[p - 1, a, 1], sibling),
        ]

    def start(copies):
        for c in copies:
            c.start()

    def arrive(copies):
        for c in copies:
            c.wait_recv()

    def start_first(p):
        if not (isinstance(p, int) and p == 0):
            arrive(x_in(p))
        start(first_out(p))

    def second_own(p):
        near = isinstance(p, int) and p == 0
        k1_in(p, 0).wait_recv()
        start([k2_out(p, 0, i) for i in range(3)])
        if near:
            sk(0, 3, core).start()
        arrive([v1_in(p, i) for i in range(3)])
        v2_out(p, 0).start()
        if near:
            sv(3, core).start()
        arrive([k1_in(p, i) for i in (1, 2)])
        if near:
            sk(1, 3, core).start()

    def second_other(p):
        start([k2_out(p, 1, i) for i in range(3)])
        start([v2_out(p, i) for i in (1, 2)])

    def start_second(p):
        second_own(p)
        second_other(p)

    def share_first(a):
        for i in (1, 2, 0):
            k2_in(0, a, i).wait_recv()
            sk(a, i, core).start()
        for i in ((0,), (1, 2))[a]:
            v2_in(0, i).wait_recv()
            sv(i, core).start()
        for i in range(2):
            start(far_out(i, a))

    def have_first(a):
        arrive([sk(a, i, other) for i in range(4)])
        arrive([sv(i, other) for i in ((0, 3), (1, 2))[a]])

    def share_later(p, a):
        arrive([k2_in(p, a, i) for i in (1, 2, 0)])
        through_x = not (isinstance(p, int) and p == 3)
        if through_x:
            far_in(p, a)[0].wait_recv()
        ks, vs = share(p, a, core)
        ks.start()
        arrive([v2_in(p, i) for i in ((0,), (1, 2))[a]])
        if through_x:
            far_in(p, a)[1].wait_recv()
        vs.start()

    def have_later(p, a):
        arrive(share(p, a, other))

    start_first(0)
    for i in range(3):
        start(x_out(i))

    key_at = lax.broadcasted_iota(jnp.int32, (TOKENS, ROWS), 0)
    token_at = lax.broadcasted_iota(jnp.int32, (TOKENS, ROWS), 1) % TOKENS
    mask_ref[...] = jnp.where(token_at >= key_at, 0.0, -jnp.inf).astype(jnp.float32)
    length = lengths_ref[0]

    def columns(g, hh, h):
        return pl.ds(pl.multiple_of((g * GROUP + hh * HALF + h) * D, D), D)

    def queries(g, t):
        hh, j = t // 3, t % 3
        q = jnp.concatenate([q_ref[j * TOKENS : (j + 1) * TOKENS, columns(g, hh, h)] for h in range(HALF)], axis=0)
        q = q.astype(jnp.float32) * SCALE
        high = q.astype(jnp.bfloat16)
        low = (q - high.astype(jnp.float32)).astype(jnp.bfloat16)
        return jnp.concatenate([high, low], axis=1)

    def own_head(g, carry):
        cols = pl.ds(pl.multiple_of(g * D, D), D)
        turned = ov_ref[:, cols].T
        keys = ok_ref[:, cols]
        keys = jnp.concatenate([keys, keys], axis=1)
        mask = mask_ref[...]
        scored = []
        for t in range(TILES):
            j = t % 3
            s = dot_t(keys[: (j + 1) * TOKENS], queries(g, t))
            last = s[j * TOKENS :] + mask
            scored.append(jnp.concatenate([s[: j * TOKENS], last], axis=0) if j else last)
        weighed = []
        for t in range(TILES):
            n = (t % 3 + 1) * TOKENS
            s = scored[t]
            top = jnp.max(s, axis=0, keepdims=True)
            p = jnp.exp2(s - top)
            state_ref[g * TILES + t, 0] = jnp.broadcast_to(top, (8, ROWS))
            state_ref[g * TILES + t, 1] = jnp.sum(p.reshape(n // 8, 8, ROWS), axis=0)
            weighed.append(p.astype(jnp.bfloat16))
        for t in range(TILES):
            n = (t % 3 + 1) * TOKENS
            acc_ref[g * TILES + t] = jnp.dot(turned[:, :n], weighed[t], preferred_element_type=jnp.float32)
        return carry

    def key_blocks(xp, hd, side):
        cores = range(2) if side is None else (side,)
        return [kbuf[xp, hd, c, zz, hh] for c in cores for zz in range(4) for hh in range(2)]

    def value_blocks(xp, hd, side):
        cores = range(2) if side is None else (side,)
        return [vbuf[xp, hd, c, hh, zz] for c in cores for zz in range(4) for hh in range(2)]

    per = CHUNK // D

    def scores(p, a, t, slot, side=None):
        xp, hd = plane(p), head(a)
        g = xp * 2 + hd
        q = queries(g, t)
        blocks = key_blocks(xp, hd, side)
        top = state_ref[g * TILES + t, 0]
        for c in range(len(blocks) // per):
            keys = jnp.concatenate(blocks[c * per : (c + 1) * per], axis=0)
            s = dot_t(jnp.concatenate([keys, keys], axis=1), q)
            s_ref[slot, c * CHUNK : (c + 1) * CHUNK] = s
            top = jnp.maximum(top, jnp.max(s.reshape(CHUNK // 8, 8, ROWS), axis=0))
        m_ref[slot] = jnp.broadcast_to(jnp.max(top, axis=0, keepdims=True), (8, ROWS))

    def values(p, a, t, slot, side=None, last=True):
        xp, hd = plane(p), head(a)
        g = xp * 2 + hd
        hh, j = t // 3, t % 3
        blocks = value_blocks(xp, hd, side)
        top = m_ref[slot]
        shrink = jnp.exp2(state_ref[g * TILES + t, 0] - top)
        total = state_ref[g * TILES + t, 1] * shrink
        acc = acc_ref[g * TILES + t] * shrink[:1]
        for c in range(len(blocks) // per):
            w = jnp.exp2(s_ref[slot, c * CHUNK : (c + 1) * CHUNK] - top[:1])
            total = total + jnp.sum(w.reshape(CHUNK // 8, 8, ROWS), axis=0)
            turned = jnp.concatenate(blocks[c * per : (c + 1) * per], axis=1)
            acc = acc + jnp.dot(turned, w.astype(jnp.bfloat16), preferred_element_type=jnp.float32)
        if not last:
            acc_ref[g * TILES + t] = acc
            state_ref[g * TILES + t, 0] = top
            state_ref[g * TILES + t, 1] = total
            return
        token = lax.broadcasted_iota(jnp.int32, (1, ROWS), 1) % TOKENS + j * TOKENS
        factor = jnp.where(token < length, 1.0 / jnp.sum(total, axis=0, keepdims=True), 0.0)
        out = (acc * factor).T.astype(jnp.bfloat16)
        for h in range(HALF):
            o_ref[j * TOKENS : (j + 1) * TOKENS, columns(g, hh, h)] = out[h * TOKENS : (h + 1) * TOKENS]

    for load in loads[3:]:
        load.wait()
    lax.fori_loop(0, 4, own_head, 0)
    second_own(0)
    start_first(1)
    lax.fori_loop(4, HEADS_KV, own_head, 0)
    share_first(0)
    second_other(0)

    halves = [(a, t, side) for a in range(2) for side in range(2) for t in range(TILES)]
    cores = (core, other)

    def work_first():
        for v, (a, t, side) in enumerate(halves):
            if v == 5:
                have_first(0)
                start_first(2)
                start_first(3)
            if v == 3:
                second_own(1)
            if v == 8:
                second_other(1)
            if v == 11:
                share_first(1)
            if v == 14:
                start_second(2)
            if v == 21:
                start_second(3)
            if v == 17:
                have_first(1)
            if v == 18:
                share_later(1, 0)
            if v == 23:
                have_later(1, 0)
                scores(1, 0, 0, 0)
            else:
                aa, tt, ss = halves[v + 1]
                scores(0, aa, tt, (v + 1) % 2, cores[ss])
            values(0, a, t, v % 2, cores[side], side == 1)

    scores(0, 0, 0, 0, core)

    def work(p, place):
        for u in range(2 * TILES):
            a, t = u // TILES, u % TILES
            if u == 0:
                share_later(p, 1)
            if u == 5:
                have_later(p, 1)
            if place == 1 and u == 6:
                for was in (1, 2):
                    @pl.when(p == was)
                    def _():
                        share_later(was + 1, 0)
            if place < 2 and u == 11:
                have_later(p + 1, 0)
            if u < 11:
                scores(p, (u + 1) // TILES, (u + 1) % TILES, (u + 1) % 2)
            elif place < 2:
                scores(p + 1, 0, 0, 0)
            values(p, a, t, u % 2)

    def planes(p, carry):
        work(p, 1)
        return carry

    work_first()
    lax.fori_loop(1, 3, planes, 0)
    work(3, 2)

    def sent(copies):
        for c in copies:
            c.wait_send()

    def settle(p):
        sent(first_out(p))
        for i in range(3):
            sent([k2_out(p, a, i) for a in range(2)])
            v2_out(p, i).wait_send()

    for i in range(3):
        sent(x_out(i))
        for a in range(2):
            if i < 2:
                sent(far_out(i, a))
    for i in range(4):
        sent([sk(0, i, core), sk(1, i, core), sv(i, core)])
    settle(0)

    for p in range(1, 4):
        settle(p)
        for a in range(2):
            sent(share(p, a, core))


def body(queries, own_keys, own_values, key_codes, value_codes, code_scales, lengths):
    scales = jnp.transpose(code_scales[:, 0, :])
    vmem = pl.BlockSpec(memory_space=pltpu.VMEM)
    hbm = pl.BlockSpec(memory_space=pl.ANY)
    dma = pltpu.SemaphoreType.DMA
    width = HEADS_KV * GROUP * D
    out = pl.pallas_call(
        attend,
        out_shape=pltpu.VMEM((LENGTH, width), jnp.bfloat16),
        in_specs=[hbm, hbm, hbm, pl.BlockSpec(memory_space=pltpu.SMEM), hbm, hbm, hbm],
        out_specs=vmem,
        scratch_shapes=[
            pltpu.VMEM((D, D), jnp.bfloat16),
            pltpu.VMEM((D, D), jnp.bfloat16),
            pltpu.VMEM((2, D), jnp.bfloat16),
            pltpu.VMEM((LENGTH, width), jnp.bfloat16),
            pltpu.VMEM((LENGTH, HEADS_KV * D), jnp.bfloat16),
            pltpu.VMEM((LENGTH, HEADS_KV * D), jnp.bfloat16),
            pltpu.VMEM((4, 2, 2, 4, 2, D, D), jnp.bfloat16),
            pltpu.VMEM((4, 2, 2, 2, 4, D, D), jnp.bfloat16),
            pltpu.VMEM((2, PROMPT, ROWS), jnp.float32),
            pltpu.VMEM((2, 8, ROWS), jnp.float32),
            pltpu.VMEM((TOKENS, ROWS), jnp.float32),
            pltpu.VMEM((HEADS_KV * TILES, D, ROWS), jnp.float32),
            pltpu.VMEM((HEADS_KV * TILES, 2, 8, ROWS), jnp.float32),
            dma((6,)),
            dma((3, 2)), dma((3, 2)),
            dma((2, 2, 2)), dma((2, 2, 2)),
            dma((4, 3)), dma((4, 3)),
            dma((4, 3)), dma((4, 3)),
            dma((4, 2, 3)), dma((4, 2, 3)),
            dma((4, 3)), dma((4, 3)),
            dma((2, 4)), dma((2, 4)),
            dma((4,)), dma((4,)),
            dma((3, 2, 2)), dma((3, 2, 2)),
        ],
        compiler_params=pltpu.CompilerParams(
            collective_id=0, has_side_effects=True, vmem_limit_bytes=56 * 2**20
        ),
        cost_estimate=pl.CostEstimate(flops=14_000_000_000, bytes_accessed=8_000_000, transcendentals=27_000_000),
    )(scales, key_codes, value_codes, lengths, queries[0], own_keys[0], own_values[0])
    return out[None]


def solution(mesh):
    placed = (
        P(("blk", "uly"), None, None),
        P(("blk", "uly"), None, None),
        P(("blk", "uly"), None, None),
        P("blk", "uly"),
        P("blk", "uly"),
        P("blk", "uly", None),
        P(("blk", "uly")),
    )
    return jax.shard_map(
        body, mesh=mesh, in_specs=placed, out_specs=P(("blk", "uly"), None, None), check_vma=False
    )
```
